768 devices in a mesh: dp: 192 (over y, z_lo, x), width: 4 (over z_hi, core).
Axes of the slice: x: 4, y: 8, z: 12 (z_hi: 2, z_lo: 6; z = z_hi * 6 + z_lo), core: 2. Of those that a mesh axis runs over, the one named last changes fastest.
Arguments:
- image_embed: bfloat16 [73728, 1152], P('dp', 'width'), may hold values from -0.17675781 to 0.17675781
- text_embed: bfloat16 [73728, 1152], P('dp', 'width'), may hold values from -0.17675781 to 0.17675781
- logit_scale: float32 [1], replicated, may hold values from 2 to 8
- logit_bias: float32 [1], replicated, may hold values from -3 to 0
Outputs:
- image_grad: float32 [73728, 1152], P('dp', 'width')
- text_grad: float32 [73728, 1152], P('dp', 'width')
The draws below stay inside these ranges and needn't reach their ends.
All inputs are finite; a program needn't handle non-finite values.
Results may differ from the reference program's by a relative error of at most 0.0028.
Values may be sent and summed in bfloat16 or wider, within the bound.
No kernel may reach another device: no remote copies, remote signals or barrier semaphores. Data moves between devices by JAX's collectives and lax.ppermute only.
A program may use at most 32 MiB of HBM per device.

```python
import math
import jax
import jax.numpy as jnp
from jax import lax

D = 1152
ROWS = 384
STEPS = 4
BATCH = 73728
N_DP = 192


def block_levels(rng, dims, shards, low, top_value):
    def one(position, shards_of):
        steps = jax.random.uniform(jax.random.fold_in(jax.random.fold_in(rng, 6), position), (shards_of,), jnp.float32, low / len(shards), top_value / len(shards))
        return jnp.repeat(jnp.exp(steps), dims[position] // shards_of).reshape((-1,) + (1,) * (len(dims) - position - 1))

    loudness = one(*shards[0])
    for cut in shards[1:]:
        loudness = loudness * one(*cut)
    return loudness


def gaussian(key, dims, scale, bound, cuts=(), held_as=jnp.bfloat16):
    factor_of = block_levels(key, dims, cuts, -0.22, 0.18) if cuts else 1.0
    array = jax.random.normal(key, dims, jnp.float32) * scale * factor_of
    return jnp.minimum(jnp.maximum(array, -bound), bound).astype(held_as)


def setup_inputs(seed: int = 0) -> dict:
    seeds = jax.random.split(jax.random.key(seed), 5)
    return {
        "image_embed": gaussian(seeds[0], (BATCH, D), (D ** -0.5), 0.17675781, ((0, 192), (1, 4))),
        "text_embed": gaussian(seeds[1], (BATCH, D), (D ** -0.5), 0.17675781, ((0, 192), (1, 4))),
        "logit_scale": jnp.clip(jnp.exp(jax.random.uniform(seeds[2], (1,), jnp.float32, math.log(2.0), math.log(8.0))), 2.0, 8.0),
        "logit_bias": jnp.clip(jax.random.uniform(seeds[3], (1,), jnp.float32, -3.0, 0.0), -3.0, 0.0),
    }


def reference(image_embed, text_embed, logit_scale, logit_bias):
    temper = logit_scale[0]
    offset = logit_bias[0]
    images = image_embed.reshape(N_DP, ROWS, D)
    texts = text_embed.reshape(N_DP, ROWS, D)
    identity = jnp.eye(ROWS, dtype=jnp.float32)

    def per_block(index):
        image_rows = lax.dynamic_index_in_dim(images, index, 0, False)
        image_total = jnp.zeros((ROWS, D), jnp.float32)
        pieces = []
        for step in range(STEPS):
            other = ((index - step) % N_DP).astype(jnp.int32)
            text_rows = lax.dynamic_index_in_dim(texts, other, 0, False)
            logits = temper * jnp.dot(image_rows, text_rows.T, preferred_element_type=jnp.float32) + offset
            target = identity if step == 0 else jnp.zeros_like(identity)
            weights = (temper * (jax.nn.sigmoid(logits) - target)).astype(jnp.bfloat16)
            image_total = image_total + jnp.dot(weights, text_rows, preferred_element_type=jnp.float32)
            pieces.append(jnp.dot(weights.T, image_rows, preferred_element_type=jnp.float32))
        return image_total, jnp.stack(pieces)

    image_blocks, text_terms = lax.map(per_block, jnp.arange(N_DP, dtype=jnp.int32))
    text_total = jnp.zeros((N_DP, ROWS, D), jnp.float32)
    for step in range(STEPS):
        text_total = text_total + jnp.roll(text_terms[:, step], -step, axis=0)
    return image_blocks.reshape(BATCH, D), text_total.reshape(BATCH, D)
```

```python
import numpy as np
import jax
import jax.numpy as jnp
from jax import lax
from jax.experimental import pallas as pl
from jax.experimental.pallas import tpu as pltpu
from jax.sharding import Mesh, PartitionSpec as P

AXES = ("y", "zl", "x", "zh", "core")
SIZES = (8, 6, 4, 2, 2)
NX = 4


def route(move):
    pairs = []
    for i, place in enumerate(np.ndindex(*SIZES)):
        goal = [a % b for a, b in zip(move(*place), SIZES)]
        pairs.append((i, int(np.ravel_multi_index(goal, SIZES))))
    return pairs


def flip(block):
    return lax.ppermute(block, AXES, route(lambda y, zl, x, zh, c: (y, zl, x, 1 - zh, c)))


def swap_cores(block):
    return lax.ppermute(block, AXES, route(lambda y, zl, x, zh, c: (y, zl, x, zh, 1 - c)))


def next_row(y, zl, x, zh, c):
    step = 1 if c == 0 else -1
    z = (zh * 6 + zl + step) % 12
    row = zl + step
    y = y + 1 if row > 5 else y - 1 if row < 0 else y
    return (y, z % 6, x, z // 6, c)


def shift_row(block):
    return lax.ppermute(block, AXES, route(next_row))


def grads_kernel(info, scalars, yo, yc, xo, xc, keep, send, yt):
    m = pl.program_id(0)
    place, row, core = info[0], info[1], info[2]
    temper, offset = scalars[0], scalars[1]
    wrapped = jnp.where(core == 0, jnp.logical_and(m > place, row == 0), jnp.logical_and(m < place, row == 5))
    side = wrapped.astype(jnp.int32)

    @pl.when(m == 0)
    def _():
        yt[0] = yo[...].T
        yt[1] = yc[...].T
        keep[...] = jnp.zeros_like(keep)
        send[...] = jnp.zeros_like(send)

    a, b = xo[0], xc[0]
    logits = jnp.dot(yt[side], a, preferred_element_type=jnp.float32)
    logits += jnp.dot(yt[1 - side], b, preferred_element_type=jnp.float32)
    logits = temper * logits + offset
    lined = lax.broadcasted_iota(jnp.int32, logits.shape, 0)
    column = lax.broadcasted_iota(jnp.int32, logits.shape, 1)
    target = jnp.where(jnp.logical_and(m == place, lined == column), 1.0, 0.0)
    weights = (temper * (jax.nn.sigmoid(logits) - target)).astype(jnp.bfloat16)

    def add(ref, which):
        rows = pl.ds(pl.multiple_of(which * 288, 16), 288)

        @pl.when(side == 0)
        def _():
            ref[...] += lax.dot_general(
                xo[0, rows, :], weights, (((1,), (1,)), ((), ())), preferred_element_type=jnp.float32
            )

        @pl.when(side == 1)
        def _():
            ref[...] += lax.dot_general(
                xc[0, rows, :], weights, (((1,), (1,)), ((), ())), preferred_element_type=jnp.float32
            )

    add(send, 1 - core)
    add(keep, core)


def grads(info, scalars, yo, yc, xo, xc):
    n, k, r = xo.shape
    whole = pl.BlockSpec((k, r), lambda m: (0, 0))
    one = pl.BlockSpec((1, k, r), lambda m: (m, 0, 0))
    out = pl.BlockSpec((k // 2, r), lambda m: (0, 0))
    smem = pl.BlockSpec(memory_space=pltpu.SMEM)
    return pl.pallas_call(
        grads_kernel,
        grid=(n,),
        in_specs=[smem, smem, whole, whole, one, one],
        out_specs=[out, out],
        out_shape=[jax.ShapeDtypeStruct((k // 2, r), jnp.float32)] * 2,
        scratch_shapes=[pltpu.VMEM((2, r, k), jnp.bfloat16)],
        compiler_params=pltpu.CompilerParams(vmem_limit_bytes=32 * 2**20),
        cost_estimate=pl.CostEstimate(
            flops=n * 2 * r * r * k * 3, bytes_accessed=n * k * r * 4, transcendentals=n * r * r
        ),
    )(info, scalars, yo, yc, xo, xc)


def on_device(image_embed, text_embed, logit_scale, logit_bias):
    place = lax.axis_index("x")
    row = lax.axis_index("zl")
    core = lax.axis_index("core")
    text = lax.all_gather(text_embed.T, "core", axis=0, tiled=True)
    image = lax.all_gather(image_embed.T, "core", axis=0, tiled=True)
    x_own = jnp.where(core == 0, text, image)
    y_own = jnp.where(core == 0, image, text)
    x_far = flip(x_own)
    slots = jnp.arange(NX)[:, None, None]
    from_next = jnp.where(core == 0, slots < place, slots > place)

    def exchange(block):
        moved = shift_row(block)
        return lax.all_to_all(jnp.where(from_next, moved, block), "x", 0, 0, tiled=True)

    xo = exchange(x_own)
    y_far = swap_cores(x_far)
    xc = exchange(x_far)
    info = jnp.stack([place, row, core]).astype(jnp.int32)
    scalars = jnp.concatenate([logit_scale, logit_bias])
    keep, send = grads(info, scalars, y_own, y_far, xo, xc)
    got = swap_cores(send)
    image_grad = jnp.where(core == 0, keep, got)
    text_grad = jnp.where(core == 0, got, keep)
    return (image_grad.T, text_grad.T)


def solution(mesh):
    split = Mesh(mesh.devices.reshape(SIZES), AXES)
    block = P(("y", "zl", "x"), ("zh", "core"))
    return jax.shard_map(
        on_device, mesh=split, in_specs=(block, block, P(), P()), out_specs=(block, block), check_vma=False
    )
```

```python
import numpy as np
import jax
import jax.numpy as jnp
from jax import lax
from jax.experimental import pallas as pl
from jax.experimental.pallas import tpu as pltpu
from jax.sharding import Mesh, PartitionSpec as P

AXES = ("y", "zl", "x", "zh", "core")
SIZES = (8, 6, 4, 2, 2)
NX = 4
STEPS = 4
F32 = jnp.float32
BF16 = jnp.bfloat16
HERE = pl.BlockSpec(memory_space=pltpu.VMEM)
SMEM = pl.BlockSpec(memory_space=pltpu.SMEM)


def send(block, move):
    pairs = []
    for i, place in enumerate(np.ndindex(*SIZES)):
        goal = [a % b for a, b in zip(move(*place), SIZES)]
        pairs.append((i, int(np.ravel_multi_index(goal, SIZES))))
    return lax.ppermute(block, AXES, pairs)


def flip(block):
    return send(block, lambda y, zl, x, zh, c: (y, zl, x, 1 - zh, c))


def swap_cores(block):
    return send(block, lambda y, zl, x, zh, c: (y, zl, x, zh, 1 - c))


def next_row(y, zl, x, zh, c):
    step = 1 if c == 0 else -1
    z = (zh * 6 + zl + step) % 12
    row = zl + step
    y = y + 1 if row > 5 else y - 1 if row < 0 else y
    return (y, z % 6, x, z // 6, c)


def along_dp(block, s):
    def move(y, zl, x, zh, c):
        to = x + s if c == 0 else x - s
        if not 0 <= to < NX:
            y, zl, x, zh, c = next_row(y, zl, x, zh, c)
        return (y, zl, to, zh, c)

    return send(block, move)


def call(kernel, args, out_shape, flops, moved, scratch=()):
    n = len(out_shape)
    return pl.pallas_call(
        kernel,
        in_specs=[SMEM, SMEM] + [HERE] * (len(args) - 2),
        out_specs=[HERE] * n,
        out_shape=out_shape,
        scratch_shapes=scratch,
        compiler_params=pltpu.CompilerParams(vmem_limit_bytes=40 * 2**20),
        cost_estimate=pl.CostEstimate(flops=flops, bytes_accessed=moved, transcendentals=0),
    )(*args)


def near_kernel(info, scalars, ya, yb, xa, xb, x1, x2, x3, logits, yt):
    k = ya.shape[0]
    yt[0], yt[1] = ya[...].T, yb[...].T
    logits[0] = dot(yt[0], xa[...]) + dot(yt[1], xb[...])
    for m, x in enumerate((x1, x2, x3), 1):

        @pl.when(info[m] == 0)
        def _():
            logits[m] = dot(yt[0], x[0:k]) + dot(yt[1], x[k : 2 * k])


def dot(a, b):
    return jnp.dot(a, b, preferred_element_type=F32)


def add_to(total, x, weights):
    total[...] += lax.dot_general(x, weights, (((1,), (1,)), ((), ())), preferred_element_type=F32)


def weights_kernel(info, scalars, near, yt, yc, xb, x1, x2, x3, *refs):
    far, (weights, total, yct, logits) = refs[:4], refs[4:]
    temper, offset = scalars[0], scalars[1]
    k, r = xb.shape
    total[...] = jnp.zeros_like(total)
    yct[0], yct[1] = yc[k : 2 * k].T, yc[0:k].T
    for m in range(STEPS):
        near_x = (None, x1, x2, x3)[m]
        far_x = far[m]
        if m == 0:
            logits[...] = near[m] + (dot(yct[0], far_x[0:k]) + dot(yct[1], far_x[k : 2 * k]))
        else:

            @pl.when(info[m] == 0)
            def _():
                logits[...] = near[m] + (dot(yct[0], far_x[0:k]) + dot(yct[1], far_x[k : 2 * k]))

            @pl.when(info[m] == 1)
            def _():
                logits[...] = (dot(yct[0], near_x[0:k]) + dot(yct[1], near_x[k : 2 * k])) + (
                    dot(yt[0], far_x[0:k]) + dot(yt[1], far_x[k : 2 * k])
                )

        value = jax.nn.sigmoid(temper * logits[...] + offset)
        if m == 0:
            lined = lax.broadcasted_iota(jnp.int32, (r, r), 0)
            column = lax.broadcasted_iota(jnp.int32, (r, r), 1)
            value = value - jnp.where(lined == column, 1.0, 0.0)
        weights[m] = (temper * value).astype(BF16)
        if m == 0:
            add_to(total, xb[...], weights[m])
        else:

            @pl.when(info[m] == 0)
            def _():
                add_to(total, near_x[k : 2 * k], weights[m])

            @pl.when(info[m] == 1)
            def _():
                add_to(total, far_x[k : 2 * k], weights[m])


def keep_kernel(info, scalars, weights, xa, x1, x2, x3, xc1, xc2, xc3, total):
    k, r = xa.shape
    total[...] = jnp.zeros_like(total)
    add_to(total, xa[...], weights[0])
    for m, (near_x, far_x) in enumerate(((x1, xc1), (x2, xc2), (x3, xc3)), 1):

        @pl.when(info[m] == 0)
        def _():
            add_to(total, near_x[0:k], weights[m])

        @pl.when(info[m] == 1)
        def _():
            add_to(total, far_x[0:k], weights[m])


def on_device(image_embed, text_embed, logit_scale, logit_bias):
    place = lax.axis_index("x")
    row = lax.axis_index("zl")
    core = lax.axis_index("core")
    text, image = text_embed.T, image_embed.T
    k, r = text.shape
    xa = jnp.where(core == 0, text, image)
    ya = jnp.where(core == 0, image, text)
    with jax.named_scope("cross_a"):
        xca = flip(xa)
    with jax.named_scope("share"):
        other = swap_cores(jnp.concatenate([ya, xa], axis=0))
    xb, yb = other[:k], other[k:]
    with jax.named_scope("cross_b"):
        xcb = flip(xb)
    own = jnp.concatenate([xa, xb], axis=0)
    near_x = []
    for s in range(1, STEPS):
        with jax.named_scope("near"):
            near_x.append(along_dp(own, s))
    xc = jnp.concatenate([xca, xcb], axis=0)
    far_x = [xc]
    for s in range(1, STEPS):
        with jax.named_scope("far"):
            far_x.append(along_dp(xc, s))
    with jax.named_scope("share_far"):
        yc = swap_cores(xc)

    came = [jnp.where(core == 0, place - s < 0, place + s >= NX) for s in range(STEPS)]
    edge = jnp.where(core == 0, row == 0, row == 5)
    info = jnp.stack([jnp.logical_and(c, edge) for c in came]).astype(jnp.int32)
    scalars = jnp.concatenate([logit_scale, logit_bias])
    logits = jax.ShapeDtypeStruct((STEPS, r, r), F32)
    work = 2 * STEPS * k * r * r
    near, yt = call(
        near_kernel,
        (info, scalars, ya, yb, xa, xb, *near_x),
        [logits, jax.ShapeDtypeStruct((2, r, k), BF16)],
        2 * work,
        STEPS * r * (4 * r + 4 * k),
    )
    weights, total = call(
        weights_kernel,
        (info, scalars, near, yt, yc, xb, *near_x, *far_x),
        [jax.ShapeDtypeStruct((STEPS, r, r), BF16), jax.ShapeDtypeStruct((k, r), F32)],
        3 * work,
        STEPS * r * (8 * r + 8 * k),
        [pltpu.VMEM((2, r, k), BF16), pltpu.VMEM((r, r), F32)],
    )
    with jax.named_scope("give"):
        got = swap_cores(total)
    (keep,) = call(
        keep_kernel,
        (info, scalars, weights, xa, *near_x, *far_x[1:]),
        [jax.ShapeDtypeStruct((k, r), F32)],
        work,
        STEPS * r * (2 * r + 4 * k),
    )
    image_grad = jnp.where(core == 0, keep, got)
    text_grad = jnp.where(core == 0, got, keep)
    return (image_grad.T, text_grad.T)


def solution(mesh):
    split = Mesh(mesh.devices.reshape(SIZES), AXES)
    block = P(("y", "zl", "x"), ("zh", "core"))
    return jax.shard_map(
        on_device, mesh=split, in_specs=(block, block, P(), P()), out_specs=(block, block), check_vma=False
    )
```

```python
import functools

import numpy as np
import jax
import jax.numpy as jnp
from jax import lax
from jax.experimental import pallas as pl
from jax.experimental.pallas import tpu as pltpu
from jax.sharding import Mesh, PartitionSpec as P

AXES = ("y", "zl", "x", "zh", "core")
SIZES = (8, 6, 4, 2, 2)
NX = 4
STEPS = 4
F32 = jnp.float32
BF16 = jnp.bfloat16
HERE = pl.BlockSpec(memory_space=pltpu.VMEM)
SMEM = pl.BlockSpec(memory_space=pltpu.SMEM)


def send(block, move):
    pairs = []
    for i, place in enumerate(np.ndindex(*SIZES)):
        goal = [a % b for a, b in zip(move(*place), SIZES)]
        pairs.append((i, int(np.ravel_multi_index(goal, SIZES))))
    return lax.ppermute(block, AXES, pairs)


def flip(block):
    return send(block, lambda y, zl, x, zh, c: (y, zl, x, 1 - zh, c))


def swap_cores(block):
    return send(block, lambda y, zl, x, zh, c: (y, zl, x, zh, 1 - c))


def next_row(y, zl, x, zh, c):
    step = 1 if c == 0 else -1
    z = (zh * 6 + zl + step) % 12
    row = zl + step
    y = y + 1 if row > 5 else y - 1 if row < 0 else y
    return (y, z % 6, x, z // 6, c)


def along_dp(block, s):
    def move(y, zl, x, zh, c):
        to = x + s if c == 0 else x - s
        if not 0 <= to < NX:
            y, zl, x, zh, c = next_row(y, zl, x, zh, c)
        return (y, zl, to, zh, c)

    return send(block, move)


def call(kernel, numbers, arrays, out_shape, flops, scratch=()):
    moved = sum(x.size * x.dtype.itemsize for x in (*arrays, *out_shape))
    return pl.pallas_call(
        kernel,
        in_specs=[SMEM] * len(numbers) + [HERE] * len(arrays),
        out_specs=[HERE] * len(out_shape),
        out_shape=out_shape,
        scratch_shapes=scratch,
        compiler_params=pltpu.CompilerParams(vmem_limit_bytes=16 * 2**20),
        cost_estimate=pl.CostEstimate(flops=flops, bytes_accessed=moved, transcendentals=0),
    )(*numbers, *arrays)


def dot(a, b):
    return jnp.dot(a, b, preferred_element_type=F32)


def halves(y, x):
    k = y.shape[2]
    return dot(y[0], x[0:k]) + dot(y[1], x[k : 2 * k])


def grad_term(x, weights):
    return lax.dot_general(x, weights, (((1,), (1,)), ((), ())), preferred_element_type=F32)


def near_kernel(info, ya, yb, x1, x2, x3, logits, yt):
    yt[0], yt[1] = ya[...].T, yb[...].T
    for m, x in enumerate((x1, x2, x3), 1):

        @pl.when(info[m] == 0)
        def _():
            logits[m - 1] = halves(yt, x)


def own_kernel(scalars, yt, yc, xa, xb, xc, keep, give, yct):
    k, r = xa.shape
    yct[0], yct[1] = yc[k : 2 * k].T, yc[0:k].T
    logits = dot(yt[0], xa[...]) + dot(yt[1], xb[...]) + halves(yct, xc)
    lined = lax.broadcasted_iota(jnp.int32, (r, r), 0)
    column = lax.broadcasted_iota(jnp.int32, (r, r), 1)
    value = jax.nn.sigmoid(scalars[0] * logits + scalars[1]) - jnp.where(lined == column, 1.0, 0.0)
    weights = (scalars[0] * value).astype(BF16)
    keep[...] = grad_term(xa[...], weights)
    give[...] = grad_term(xb[...], weights)


def block_kernel(m, info, scalars, near, yt, yct, near_x, far_x, *refs):
    n = 1 if len(refs) == 4 else 2
    before, totals, logits = refs[:n], refs[n : 2 * n], refs[-1]
    k = yt.shape[2]

    @pl.when(info[m] == 0)
    def _():
        logits[...] = near[m - 1] + halves(yct, far_x)

    @pl.when(info[m] == 1)
    def _():
        logits[...] = halves(yct, near_x) + halves(yt, far_x)

    weights = (scalars[0] * jax.nn.sigmoid(scalars[0] * logits[...] + scalars[1])).astype(BF16)
    if n == 1:
        refs[2][...] = weights
    for i, (old, total) in enumerate(zip(before, totals)):
        rows = pl.ds(k if i == 0 else 0, k)

        @pl.when(info[m] == 0)
        def _():
            total[...] = old[...] + grad_term(near_x[rows, :], weights)

        @pl.when(info[m] == 1)
        def _():
            total[...] = old[...] + grad_term(far_x[rows, :], weights)


def keep_kernel(m, info, weights, near_x, far_x, before, total):
    k = total.shape[0]

    @pl.when(info[m] == 0)
    def _():
        total[...] = before[...] + grad_term(near_x[0:k], weights[...])

    @pl.when(info[m] == 1)
    def _():
        total[...] = before[...] + grad_term(far_x[0:k], weights[...])


def on_device(image_embed, text_embed, logit_scale, logit_bias):
    place = lax.axis_index("x")
    row = lax.axis_index("zl")
    core = lax.axis_index("core")
    text, image = text_embed.T, image_embed.T
    k, r = text.shape
    xa = jnp.where(core == 0, text, image)
    ya = jnp.where(core == 0, image, text)
    with jax.named_scope("cross_a"):
        xca = flip(xa)
    with jax.named_scope("share"):
        other = swap_cores(jnp.concatenate([ya, xa], axis=0))
    xb, yb = other[:k], other[k:]
    with jax.named_scope("cross_b"):
        xcb = flip(xb)
    own = jnp.concatenate([xa, xb], axis=0)
    near_x = []
    for s in range(1, STEPS):
        with jax.named_scope("near"):
            near_x.append(along_dp(own, s))
    xc = jnp.concatenate([xca, xcb], axis=0)
    far_x = [xc]
    for s in range(1, STEPS):
        with jax.named_scope("far"):
            far_x.append(along_dp(xc, s))
    with jax.named_scope("share_far"):
        yc = swap_cores(xc)

    came = [jnp.where(core == 0, place - s < 0, place + s >= NX) for s in range(STEPS)]
    edge = jnp.where(core == 0, row == 0, row == 5)
    info = jnp.stack([jnp.logical_and(c, edge) for c in came]).astype(jnp.int32)
    scalars = jnp.concatenate([logit_scale, logit_bias])
    square, turned = jax.ShapeDtypeStruct((r, r), BF16), jax.ShapeDtypeStruct((2, r, k), BF16)
    half = jax.ShapeDtypeStruct((k, r), F32)
    work = 2 * k * r * r
    near, yt = call(
        near_kernel,
        [info],
        [ya, yb, *near_x],
        [jax.ShapeDtypeStruct((STEPS - 1, r, r), F32), turned],
        6 * work,
    )
    keep, give, yct = call(own_kernel, [scalars], [yt, yc, xa, xb, xc], [half, half, turned], 6 * work)
    for m in (3, 2):
        give, keep = call(
            functools.partial(block_kernel, m),
            [info, scalars],
            [near, yt, yct, near_x[m - 1], far_x[m], give, keep],
            [half, half],
            4 * work,
            [pltpu.VMEM((r, r), F32)],
        )
    give, weights = call(
        functools.partial(block_kernel, 1),
        [info, scalars],
        [near, yt, yct, near_x[0], far_x[1], give],
        [half, square],
        3 * work,
        [pltpu.VMEM((r, r), F32)],
    )
    with jax.named_scope("give"):
        got = swap_cores(give)
    (keep,) = call(
        functools.partial(keep_kernel, 1), [info], [weights, near_x[0], far_x[1], keep], [half], work
    )
    image_grad = jnp.where(core == 0, keep, got)
    text_grad = jnp.where(core == 0, got, keep)
    return (image_grad.T, text_grad.T)


def solution(mesh):
    split = Mesh(mesh.devices.reshape(SIZES), AXES)
    block = P(("y", "zl", "x"), ("zh", "core"))
    return jax.shard_map(
        on_device, mesh=split, in_specs=(block, block, P(), P()), out_specs=(block, block), check_vma=False
    )
```

```python
import functools

import numpy as np
import jax
import jax.numpy as jnp
from jax import lax
from jax.experimental import pallas as pl
from jax.experimental.pallas import tpu as pltpu
from jax.sharding import Mesh, PartitionSpec as P

AXES = ("y", "zl", "x", "zh", "core")
SIZES = (8, 6, 4, 2, 2)
NX = 4
STEPS = 4
F32 = jnp.float32
BF16 = jnp.bfloat16
HERE = pl.BlockSpec(memory_space=pltpu.VMEM)
SMEM = pl.BlockSpec(memory_space=pltpu.SMEM)


def send(block, move):
    pairs = []
    for i, place in enumerate(np.ndindex(*SIZES)):
        goal = [a % b for a, b in zip(move(*place), SIZES)]
        pairs.append((i, int(np.ravel_multi_index(goal, SIZES))))
    return lax.ppermute(block, AXES, pairs)


def flip(block):
    return send(block, lambda y, zl, x, zh, c: (y, zl, x, 1 - zh, c))


def swap_cores(block):
    return send(block, lambda y, zl, x, zh, c: (y, zl, x, zh, 1 - c))


def next_row(y, zl, x, zh, c):
    step = 1 if c == 0 else -1
    z = (zh * 6 + zl + step) % 12
    row = zl + step
    y = y + 1 if row > 5 else y - 1 if row < 0 else y
    return (y, z % 6, x, z // 6, c)


def along_dp(block, s):
    def move(y, zl, x, zh, c):
        to = x + s if c == 0 else x - s
        if not 0 <= to < NX:
            y, zl, x, zh, c = next_row(y, zl, x, zh, c)
        return (y, zl, to, zh, c)

    return send(block, move)


def call(kernel, numbers, arrays, out_shape, flops, scratch=()):
    moved = sum(x.size * x.dtype.itemsize for x in (*arrays, *out_shape))
    return pl.pallas_call(
        kernel,
        in_specs=[SMEM] * len(numbers) + [HERE] * len(arrays),
        out_specs=[HERE] * len(out_shape),
        out_shape=out_shape,
        scratch_shapes=scratch,
        compiler_params=pltpu.CompilerParams(vmem_limit_bytes=16 * 2**20),
        cost_estimate=pl.CostEstimate(flops=flops, bytes_accessed=moved, transcendentals=0),
    )(*numbers, *arrays)


def dot(a, b):
    return jnp.dot(a, b, preferred_element_type=F32)


def halves(y, x):
    k = y.shape[2]
    return dot(y[0], x[0:k]) + dot(y[1], x[k : 2 * k])


def grad_term(x, weights):
    return lax.dot_general(x, weights, (((1,), (1,)), ((), ())), preferred_element_type=F32)


def near_kernel(info, ya, yb, x1, x2, x3, logits, yt):
    yt[0], yt[1] = ya[...].T, yb[...].T
    for m, x in enumerate((x1, x2, x3), 1):

        @pl.when(info[m] == 0)
        def _():
            logits[m - 1] = halves(yt, x)


def own_kernel(scalars, yt, yc, xa, xb, xc, keep, give, yct):
    k, r = xa.shape
    yct[0], yct[1] = yc[k : 2 * k].T, yc[0:k].T
    logits = dot(yt[0], xa[...]) + dot(yt[1], xb[...]) + halves(yct, xc)
    lined = lax.broadcasted_iota(jnp.int32, (r, r), 0)
    column = lax.broadcasted_iota(jnp.int32, (r, r), 1)
    value = jax.nn.sigmoid(scalars[0] * logits + scalars[1]) - jnp.where(lined == column, 1.0, 0.0)
    weights = (scalars[0] * value).astype(BF16)
    keep[...] = grad_term(xa[...], weights)
    give[...] = grad_term(xb[...], weights)


def block_kernel(m, info, scalars, near, yt, yct, near_x, far_x, *refs):
    n = 1 if len(refs) == 4 else 2
    before, totals, logits = refs[:n], refs[n : 2 * n], refs[-1]
    k = yt.shape[2]

    @pl.when(info[m] == 0)
    def _():
        logits[...] = near[m - 1] + halves(yct, far_x)

    @pl.when(info[m] == 1)
    def _():
        logits[...] = halves(yct, near_x) + halves(yt, far_x)

    weights = (scalars[0] * jax.nn.sigmoid(scalars[0] * logits[...] + scalars[1])).astype(BF16)
    if n == 1:
        refs[2][...] = weights
    for i, (old, total) in enumerate(zip(before, totals)):
        rows = pl.ds(k if i == 0 else 0, k)

        @pl.when(info[m] == 0)
        def _():
            total[...] = old[...] + grad_term(near_x[rows, :], weights)

        @pl.when(info[m] == 1)
        def _():
            total[...] = old[...] + grad_term(far_x[rows, :], weights)


def keep_kernel(m, info, weights, near_x, far_x, before, total):
    k = total.shape[0]

    @pl.when(info[m] == 0)
    def _():
        total[...] = before[...] + grad_term(near_x[0:k], weights[...])

    @pl.when(info[m] == 1)
    def _():
        total[...] = before[...] + grad_term(far_x[0:k], weights[...])


def on_device(image_embed, text_embed, logit_scale, logit_bias):
    place = lax.axis_index("x")
    row = lax.axis_index("zl")
    core = lax.axis_index("core")
    text, image = text_embed.T, image_embed.T
    k, r = text.shape
    xa = jnp.where(core == 0, text, image)
    ya = jnp.where(core == 0, image, text)
    with jax.named_scope("cross_a"):
        xca = flip(xa)
    with jax.named_scope("share"):
        other = lax.cond(place >= 0, swap_cores, lambda b: b, jnp.concatenate([ya, xa], axis=0))
    xb, yb = other[:k], other[k:]
    with jax.named_scope("cross_b"):
        xcb = flip(xb)
    own = jnp.concatenate([xa, xb], axis=0)
    near_x = []
    for s in range(1, STEPS):
        with jax.named_scope("near"):
            near_x.append(along_dp(own, s))
    xc = jnp.concatenate([xca, xcb], axis=0)
    far_x = [xc]
    for s in range(1, STEPS):
        with jax.named_scope("far"):
            far_x.append(along_dp(xc, s))
    with jax.named_scope("share_far"):
        yc = swap_cores(xc)

    came = [jnp.where(core == 0, place - s < 0, place + s >= NX) for s in range(STEPS)]
    edge = jnp.where(core == 0, row == 0, row == 5)
    info = jnp.stack([jnp.logical_and(c, edge) for c in came]).astype(jnp.int32)
    scalars = jnp.concatenate([logit_scale, logit_bias])
    square, turned = jax.ShapeDtypeStruct((r, r), BF16), jax.ShapeDtypeStruct((2, r, k), BF16)
    half = jax.ShapeDtypeStruct((k, r), F32)
    work = 2 * k * r * r
    near, yt = call(
        near_kernel,
        [info],
        [ya, yb, *near_x],
        [jax.ShapeDtypeStruct((STEPS - 1, r, r), F32), turned],
        6 * work,
    )
    keep, give, yct = call(own_kernel, [scalars], [yt, yc, xa, xb, xc], [half, half, turned], 6 * work)
    for m in (3, 2):
        give, keep = call(
            functools.partial(block_kernel, m),
            [info, scalars],
            [near, yt, yct, near_x[m - 1], far_x[m], give, keep],
            [half, half],
            4 * work,
            [pltpu.VMEM((r, r), F32)],
        )
    give, weights = call(
        functools.partial(block_kernel, 1),
        [info, scalars],
        [near, yt, yct, near_x[0], far_x[1], give],
        [half, square],
        3 * work,
        [pltpu.VMEM((r, r), F32)],
    )
    with jax.named_scope("give"):
        got = swap_cores(give)
    (keep,) = call(
        functools.partial(keep_kernel, 1), [info], [weights, near_x[0], far_x[1], keep], [half], work
    )
    image_grad = jnp.where(core == 0, keep, got)
    text_grad = jnp.where(core == 0, got, keep)
    return (image_grad.T, text_grad.T)


def solution(mesh):
    split = Mesh(mesh.devices.reshape(SIZES), AXES)
    block = P(("y", "zl", "x"), ("zh", "core"))
    return jax.shard_map(
        on_device, mesh=split, in_specs=(block, block, P(), P()), out_specs=(block, block), check_vma=False
    )
```

```python
import functools

import numpy as np
import jax
import jax.numpy as jnp
from jax import lax
from jax.experimental import pallas as pl
from jax.experimental.pallas import tpu as pltpu
from jax.sharding import Mesh, PartitionSpec as P

AXES = ("y", "zl", "x", "zh", "core")
SIZES = (8, 6, 4, 2, 2)
NX = 4
STEPS = 4
F32 = jnp.float32
BF16 = jnp.bfloat16
HERE = pl.BlockSpec(memory_space=pltpu.VMEM)
SMEM = pl.BlockSpec(memory_space=pltpu.SMEM)


def send(block, move):
    pairs = []
    for i, place in enumerate(np.ndindex(*SIZES)):
        goal = [a % b for a, b in zip(move(*place), SIZES)]
        pairs.append((i, int(np.ravel_multi_index(goal, SIZES))))
    return lax.ppermute(block, AXES, pairs)


def after(value, other):
    return lax.optimization_barrier((value, other))[0]


def flip(block):
    return send(block, lambda y, zl, x, zh, c: (y, zl, x, 1 - zh, c))


def swap_cores(block):
    return send(block, lambda y, zl, x, zh, c: (y, zl, x, zh, 1 - c))


def next_row(y, zl, x, zh, c):
    step = 1 if c == 0 else -1
    z = (zh * 6 + zl + step) % 12
    row = zl + step
    y = y + 1 if row > 5 else y - 1 if row < 0 else y
    return (y, z % 6, x, z // 6, c)


def along_dp(block, s):
    def move(y, zl, x, zh, c):
        to = x + s if c == 0 else x - s
        if not 0 <= to < NX:
            y, zl, x, zh, c = next_row(y, zl, x, zh, c)
        return (y, zl, to, zh, c)

    return send(block, move)


def call(kernel, numbers, arrays, out_shape, flops, scratch=()):
    moved = sum(x.size * x.dtype.itemsize for x in (*arrays, *out_shape))
    return pl.pallas_call(
        kernel,
        in_specs=[SMEM] * len(numbers) + [HERE] * len(arrays),
        out_specs=[HERE] * len(out_shape),
        out_shape=out_shape,
        scratch_shapes=scratch,
        compiler_params=pltpu.CompilerParams(vmem_limit_bytes=8 * 2**20),
        cost_estimate=pl.CostEstimate(flops=flops, bytes_accessed=moved, transcendentals=0),
    )(*numbers, *arrays)


def dot(a, b):
    return jnp.dot(a, b, preferred_element_type=F32)


def halves(y, x):
    k = y.shape[2]
    return dot(y[0], x[0:k]) + dot(y[1], x[k : 2 * k])


def grad_term(x, weights):
    return lax.dot_general(x, weights, (((1,), (1,)), ((), ())), preferred_element_type=F32)


def near_kernel(info, ya, yb, x1, x2, x3, logits, yt):
    yt[0], yt[1] = ya[...].T, yb[...].T
    for m, x in enumerate((x1, x2, x3), 1):

        @pl.when(info[m] == 0)
        def _():
            logits[m - 1] = halves(yt, x)


def own_kernel(scalars, yt, yc, xa, xb, xc, keep, give, yct):
    k, r = xa.shape
    yct[0], yct[1] = yc[k : 2 * k].T, yc[0:k].T
    logits = dot(yt[0], xa[...]) + dot(yt[1], xb[...]) + halves(yct, xc)
    lined = lax.broadcasted_iota(jnp.int32, (r, r), 0)
    column = lax.broadcasted_iota(jnp.int32, (r, r), 1)
    value = jax.nn.sigmoid(scalars[0] * logits + scalars[1]) - jnp.where(lined == column, 1.0, 0.0)
    weights = (scalars[0] * value).astype(BF16)
    keep[...] = grad_term(xa[...], weights)
    give[...] = grad_term(xb[...], weights)


def block_kernel(m, info, scalars, near, yt, yct, near_x, far_x, *refs):
    n = 1 if len(refs) == 4 else 2
    before, totals, logits = refs[:n], refs[n : 2 * n], refs[-1]
    k = yt.shape[2]

    @pl.when(info[m] == 0)
    def _():
        logits[...] = near[m - 1] + halves(yct, far_x)

    @pl.when(info[m] == 1)
    def _():
        logits[...] = halves(yct, near_x) + halves(yt, far_x)

    weights = (scalars[0] * jax.nn.sigmoid(scalars[0] * logits[...] + scalars[1])).astype(BF16)
    if n == 1:
        refs[2][...] = weights
    for i, (old, total) in enumerate(zip(before, totals)):
        rows = pl.ds(k if i == 0 else 0, k)

        @pl.when(info[m] == 0)
        def _():
            total[...] = old[...] + grad_term(near_x[rows, :], weights)

        @pl.when(info[m] == 1)
        def _():
            total[...] = old[...] + grad_term(far_x[rows, :], weights)


def keep_kernel(m, info, weights, near_x, far_x, before, total):
    k = total.shape[0]

    @pl.when(info[m] == 0)
    def _():
        total[...] = before[...] + grad_term(near_x[0:k], weights[...])

    @pl.when(info[m] == 1)
    def _():
        total[...] = before[...] + grad_term(far_x[0:k], weights[...])


def on_device(image_embed, text_embed, logit_scale, logit_bias):
    place = lax.axis_index("x")
    row = lax.axis_index("zl")
    core = lax.axis_index("core")
    text, image = text_embed.T, image_embed.T
    k, r = text.shape
    xa = jnp.where(core == 0, text, image)
    ya = jnp.where(core == 0, image, text)
    with jax.named_scope("cross_a"):
        xca = flip(xa)
    with jax.named_scope("share"):
        other = lax.cond(place >= 0, swap_cores, lambda b: b, jnp.concatenate([ya, xa], axis=0))
    xb, yb = other[:k], other[k:]
    with jax.named_scope("cross_b"):
        xcb = flip(xb)
    own = jnp.concatenate([xa, xb], axis=0)
    near_x = []
    for s in range(1, STEPS):
        with jax.named_scope("near"):
            near_x.append(along_dp(own, s))
    xc = jnp.concatenate([xca, xcb], axis=0)
    far_x = [xc]
    for s in range(1, STEPS):
        with jax.named_scope("far"):
            far_x.append(along_dp(xc, s))
    with jax.named_scope("share_far"):
        yc = swap_cores(after(xc, near_x[0]))

    came = [jnp.where(core == 0, place - s < 0, place + s >= NX) for s in range(STEPS)]
    edge = jnp.where(core == 0, row == 0, row == 5)
    info = jnp.stack([jnp.logical_and(c, edge) for c in came]).astype(jnp.int32)
    scalars = jnp.concatenate([logit_scale, logit_bias])
    square, turned = jax.ShapeDtypeStruct((r, r), BF16), jax.ShapeDtypeStruct((2, r, k), BF16)
    half = jax.ShapeDtypeStruct((k, r), F32)
    work = 2 * k * r * r
    near, yt = call(
        near_kernel,
        [info],
        [ya, yb, *near_x],
        [jax.ShapeDtypeStruct((STEPS - 1, r, r), F32), turned],
        6 * work,
    )
    keep, give, yct = call(own_kernel, [scalars], [yt, yc, xa, xb, xc], [half, half, turned], 6 * work)
    *others, last = 3, 2, 1
    for m in others:
        give, keep = call(
            functools.partial(block_kernel, m),
            [info, scalars],
            [near, yt, yct, near_x[m - 1], far_x[m], give, keep],
            [half, half],
            4 * work,
            [pltpu.VMEM((r, r), F32)],
        )
    give, weights = call(
        functools.partial(block_kernel, last),
        [info, scalars],
        [near, yt, yct, near_x[last - 1], far_x[last], give],
        [half, square],
        3 * work,
        [pltpu.VMEM((r, r), F32)],
    )
    with jax.named_scope("give"):
        got = swap_cores(give)
    (keep,) = call(
        functools.partial(keep_kernel, last), [info], [weights, near_x[last - 1], far_x[last], keep], [half], work
    )
    image_grad = jnp.where(core == 0, keep, got)
    text_grad = jnp.where(core == 0, got, keep)
    return (image_grad.T, text_grad.T)


def solution(mesh):
    split = Mesh(mesh.devices.reshape(SIZES), AXES)
    block = P(("y", "zl", "x"), ("zh", "core"))
    return jax.shard_map(
        on_device, mesh=split, in_specs=(block, block, P(), P()), out_specs=(block, block), check_vma=False
    )
```
